256 devices in a mesh: section: 8 (over y_hi, x), ed: 32 (over y_lo, z, core).
Axes of the slice: x: 4, y: 4 (y_hi: 2, y_lo: 2; y = y_hi * 2 + y_lo), z: 8, core: 2. Of those that a mesh axis runs over, the one named last changes fastest.
Arguments:
- hidden: bfloat16 [512, 7168], P('ed'), may hold values from -24 to 24
- moe_gain: bfloat16 [7168], replicated, may hold values from 0.25 to 1.75
- expert_ids: int32 [512, 4], P('ed'), may hold values from 0 to 31, all different within a row; in each aligned block of 16 rows (0 to 15, 16 to 31, ...) at most 4 rows name the same one
- gate_weights: float32 [512, 4], P('ed'), may hold values from 0.1 to 1
- gate_matrix: bfloat16 [32, 7168, 1024], P('ed', None, 'section'), may hold values from -0.0625 to 0.0625
- up_matrix: bfloat16 [32, 7168, 1024], P('ed', None, 'section'), may hold values from -0.0625 to 0.0625
- down_matrix: bfloat16 [32, 1024, 7168], P('ed', 'section'), may hold values from -0.1875 to 0.1875
- head_gain: bfloat16 [7168], replicated, may hold values from 0.25 to 1.75
- head_table: bfloat16 [65536, 7168], P(('section', 'ed')), may hold values from -16 to 16
- targets: int32 [512], replicated, may hold values from 0 to 65535
- loss_weight: float32 [512], replicated, may hold values from 0.25 to 1
Outputs:
- block_out: bfloat16 [512, 7168], P('ed')
- loss: float32 [512], replicated
- head_grad: bfloat16 [65536, 7168], P(('section', 'ed'))
The draws below stay inside these ranges and needn't reach their ends.
Inputs may be any that keep to these rules, and one draw needn't show every extreme that they name: `expert_ids`: each row names 4 different experts; the tokens of one index of ed name one expert 4 times at most.
All inputs are finite; a program needn't handle non-finite values.
Results may differ from the reference program's by a relative error of at most 0.015.
Values may be sent and summed in bfloat16 or wider, within the bound.
No kernel may reach another device: no remote copies, remote signals or barrier semaphores. Data moves between devices by JAX's collectives and lax.ppermute only.
A program may use at most 128 MiB of HBM per device.

```python
import math
import jax
import jax.numpy as jnp
import numpy as np
from jax import lax

D = 7168
EH = 1024
VOC_DEV = 256
TOK_ED = 16
TOP = 4
TOKENS = 512
EXPERTS = 32
CAP = 4
VOCAB = 65536
N_SECTION = 8
N_ED = 32


def shared_direction(key):
    return jnp.clip(jax.random.normal(jax.random.fold_in(key, 97), (1, D)), -1.5, 1.5)


def draw_hidden(key, part):
    direction = shared_direction(key)
    key = jax.random.fold_in(key, 11)
    key_rows = jax.random.fold_in(key, 0)
    key_cols = jax.random.fold_in(key, 1)
    key_main = jax.random.fold_in(key, 2)
    key_align = jax.random.fold_in(key, 4)
    row_scale = jnp.exp(jax.random.uniform(key_rows, (TOKENS, 1), minval=math.log(0.3), maxval=math.log(3.0)))
    col_scale = jnp.exp(jax.random.uniform(key_cols, (1, D), minval=math.log(0.3), maxval=math.log(3.0)))
    values = jax.random.normal(key_main, (TOKENS, D)) * row_scale * col_scale
    aligned = jax.random.randint(key_align, (TOKENS, 1), 0, 6) == 0
    values = jnp.where(aligned, 16.0 * direction, values)
    return jnp.clip(values, -24.0, 24.0).astype(jnp.bfloat16)


def draw_head_table(key, part):
    direction = shared_direction(key)
    key = jax.random.fold_in(key, 23)
    key_main, key_pick, key_strength, key_gap = jax.random.split(key, 4)
    values = jnp.clip(jax.random.normal(key_main, (VOCAB, D)), -6.0, 6.0) / math.sqrt(D)
    pair_chosen = jax.random.randint(key_pick, (VOCAB // 2, 1), 0, 32) == 0
    pair_strength = jax.random.uniform(key_strength, (VOCAB // 2, 1), minval=220.0, maxval=320.0)
    pair_gap = jax.random.uniform(key_gap, (VOCAB // 2, 1), minval=1.0, maxval=3.0)
    second = jnp.array([0.0, 1.0], jnp.float32).reshape(1, 2, 1)
    strength = (pair_strength[:, None, :] - second * pair_gap[:, None, :]).reshape(VOCAB, 1)
    chosen = jnp.broadcast_to(pair_chosen[:, None, :], (VOCAB // 2, 2, 1)).reshape(VOCAB, 1)
    planted = strength * direction / (0.8 * D)
    values = jnp.where(chosen, planted, values)
    return jnp.clip(values, -16.0, 16.0).astype(jnp.bfloat16)


def place_ends(entries, stream_key, least, largest):
    extent = entries.shape
    index_at = [jax.random.randint(jax.random.fold_in(stream_key, axis), (), 0, extent[axis]) for axis in range(len(extent))]
    entries = entries.at[tuple(index_at)].set(least)
    longest = extent.index(max(extent))
    index_at[longest] = (index_at[longest] + 1) % extent[longest]
    return entries.at[tuple(index_at)].set(largest)


def levels(stream_key, shape, cuts, smallest, top_value):
    gain, own = 1.0, jax.random.fold_in(stream_key, 6)
    for dim, shards_of in cuts:
        draws = jnp.exp(jax.random.uniform(jax.random.fold_in(own, dim), (shards_of,), jnp.float32, smallest / len(cuts), top_value / len(cuts)))
        gain = gain * jnp.repeat(draws, shape[dim] // shards_of).reshape([-1 if axis == dim else 1 for axis in range(len(shape))])
    return gain


def rank_bounds(number_of, lean):
    weights = [(1 << 20) // math.isqrt(grade ** lean) + 1 for grade in range(1, number_of + 1)]
    deviation = 1 + sum(weights) // (1 << 30)
    return np.cumsum(np.array([max(1, weight // deviation) for weight in weights]))


def skewed_ids(key, dims, amount, slope):
    listing = rank_bounds(amount, slope)
    ticket = jax.random.randint(jax.random.fold_in(key, 1), dims, 0, int(listing[amount - 1]))
    standing = jnp.searchsorted(jnp.asarray(listing, jnp.int32), ticket, side="right")
    return jax.random.permutation(jax.random.fold_in(key, 2), amount)[standing].astype(jnp.int32)


def routed_block(own_key, own, number, rows, count, top, most, lean):
    order = jax.random.permutation(own_key, count)
    packed, usual = portions_of(count, rows * top, most, lean, True), portions_of(count, rows * top, most, lean, False)
    places = jnp.arange(count)

    def named(lengths, rotation):
        used = int((lengths > 0).sum())
        fixed = max(1, used // 4)
        shifted = fixed + (places - fixed + rotation * (used - fixed)) % max(1, count - fixed)
        return jnp.zeros((count,), jnp.int32).at[order[jnp.where(places < fixed, places, shifted)]].set(jnp.asarray(lengths, jnp.int32))

    lengths = jnp.where(number % 4 == 0, named(packed, number // 4), named(usual, number - number // 4 - 1))
    mixed = jax.random.permutation(jax.random.fold_in(own, 3), count)
    giver, taker = mixed[0:count // 2 * 2:2], mixed[1:count // 2 * 2:2]
    room = jnp.minimum(lengths[giver] - 1, most - lengths[taker]) // 2
    room = jnp.where((giver == order[0]) | (taker == order[0]) | (lengths[taker] == 0), 0, jnp.maximum(room, 0))
    shifted = jax.random.randint(jax.random.fold_in(own, 4), (count // 2,), 0, 1 << 20) % (room + 1)
    lengths = lengths.at[giver].add(-shifted).at[taker].add(shifted)
    labels = jnp.searchsorted(jnp.cumsum(lengths), jnp.arange(rows * top), side="right").astype(jnp.int32)
    grid = labels.reshape(top, rows).T
    grid = grid[jax.random.permutation(jax.random.fold_in(own, 1), rows)]
    rotation = jax.random.randint(jax.random.fold_in(own, 2), (rows, 1), 0, top)
    return jnp.take_along_axis(grid, (jnp.arange(top)[None, :] + rotation) % top, axis=1)


def portions_of(amount, total, bound, skew, full):
    weights = [(1 << 20) // math.isqrt(standing ** skew) + 1 for standing in range(1, amount + 1)]
    largest = bound if full else min(bound, max(-(-total // amount), total * weights[0] // sum(weights)))
    least = 1 if total - largest >= amount - 1 else 0
    given, rest = [largest] + [least] * (amount - 1), total - largest - least * (amount - 1)
    while rest > 0:
        movable = [i for i in range(1, amount) if given[i] < largest] or [i for i in range(1, amount) if given[i] < bound]
        pool, left = sum([weights[i] for i in movable]), rest
        for i in movable:
            more = min(bound - given[i], max(1, left * weights[i] // pool), rest)
            given[i] = given[i] + more
            rest = rest - more
    return np.array(given)


def gaussian(stream_key, dims, width, reach, cuts=(), kind=jnp.bfloat16):
    drawn = jax.random.normal(stream_key, dims, jnp.float32) * width
    if len(cuts) > 0:
        drawn = levels(stream_key, dims, cuts, -0.22, 0.18) * drawn
    return jnp.clip(drawn, min=-reach, max=reach).astype(kind)


def setup_inputs(seed: int = 0) -> dict:
    seeds = jax.random.split(jax.random.key(seed), 12)
    hidden = draw_hidden(jax.random.fold_in(seeds[11], 71), 0)
    moe_gain = jnp.clip(1.0 + 0.15 * jax.random.normal(seeds[1], (D,), jnp.float32), 0.25, 1.75).astype(jnp.bfloat16)
    expert_ids_keys = jax.random.split(jax.random.fold_in(seeds[2], 1), TOKENS // TOK_ED)
    expert_ids_turns = jax.random.permutation(jax.random.fold_in(seeds[2], 3), TOKENS // TOK_ED)
    expert_ids = jax.vmap(lambda own, number: routed_block(jax.random.fold_in(seeds[2], 2), own, number, TOK_ED, EXPERTS, TOP, CAP, 2))(expert_ids_keys, expert_ids_turns).reshape((TOKENS, TOP))
    gate_weights = jnp.clip(0.1 + 0.9 * jax.random.uniform(seeds[3], (TOKENS, TOP), jnp.float32) ** levels(seeds[3], (TOKENS, TOP), ((0, 32),), -0.2, 0.2), 0.1, 1.0)
    gate_matrix = gaussian(seeds[4], (EXPERTS, D, EH), D ** -0.5, 0.0625, ((0, 32), (2, 8)))
    up_matrix = gaussian(seeds[5], (EXPERTS, D, EH), D ** -0.5, 0.0625, ((0, 32), (2, 8)))
    down_matrix = gaussian(seeds[6], (EXPERTS, EH, D), EH ** -0.5, 0.1875, ((0, 32), (1, 8)))
    head_gain = jnp.clip(1.0 + 0.15 * jax.random.normal(seeds[7], (D,), jnp.float32), 0.25, 1.75).astype(jnp.bfloat16)
    head_table = draw_head_table(jax.random.fold_in(seeds[11], 71), 0)
    targets = place_ends(skewed_ids(seeds[9], (TOKENS,), VOCAB, 2), jax.random.fold_in(seeds[9], 3), 0, VOCAB - 1).astype(jnp.int32)
    loss_weight = jnp.clip(jax.random.uniform(seeds[10], (TOKENS,), jnp.float32, 0.25, 1.0), 0.25, 1.0)
    return dict(hidden=hidden, moe_gain=moe_gain, expert_ids=expert_ids, gate_weights=gate_weights, gate_matrix=gate_matrix, up_matrix=up_matrix, down_matrix=down_matrix, head_gain=head_gain, head_table=head_table, targets=targets, loss_weight=loss_weight)


def rms_scale(values, gain_vec):
    values = values.astype(jnp.float32)
    mean_square = lax.optimization_barrier(jnp.mean(values * values, axis=-1, keepdims=True))
    return values * lax.rsqrt(mean_square + 1e-06) * gain_vec.astype(jnp.float32)

def reference(hidden, moe_gain, expert_ids, gate_weights, gate_matrix, up_matrix, down_matrix, head_gain, head_table, targets, loss_weight):
    normed = rms_scale(hidden, moe_gain).astype(jnp.bfloat16)
    share_width = EH // N_SECTION

    def expert_step(running, expert):
        is_expert = expert_ids == expert
        weight = lax.optimization_barrier(jnp.sum(jnp.where(is_expert, gate_weights, 0.0), axis=1))
        is_routed = jnp.any(is_expert, axis=1).astype(jnp.int32)
        picked_rows = jnp.argsort(-is_routed, stable=True)[:N_ED * CAP].astype(jnp.int32)
        selected = normed[picked_rows]
        gate_proj = jnp.dot(selected, gate_matrix[expert], preferred_element_type=jnp.float32)
        up_proj = jnp.dot(selected, up_matrix[expert], preferred_element_type=jnp.float32)
        inner_act = (jax.nn.silu(gate_proj) * up_proj).astype(jnp.bfloat16)
        inner_shares = inner_act.astype(jnp.float32).reshape(-1, N_SECTION, share_width)
        down_shares = down_matrix[expert].astype(jnp.float32).reshape(N_SECTION, share_width, D)
        share_out = jnp.einsum('rsh,shd->rsd', inner_shares, down_shares)
        share_out = lax.optimization_barrier(share_out.astype(jnp.bfloat16)).astype(jnp.float32)
        expert_out = lax.optimization_barrier(jnp.sum(share_out, axis=1))
        running = running.at[picked_rows].add(weight[picked_rows][:, None] * expert_out)
        return (running, None)
    routed, _ = lax.scan(expert_step, jnp.zeros((TOKENS, D), jnp.float32), jnp.arange(EXPERTS, dtype=jnp.int32))
    block_out = (hidden.astype(jnp.float32) + routed).astype(jnp.bfloat16)
    head_in = rms_scale(block_out, head_gain).astype(jnp.bfloat16)
    blocks = head_table.reshape(VOCAB // VOC_DEV, VOC_DEV, D)
    indices = jnp.arange(VOCAB // VOC_DEV, dtype=jnp.int32)

    def stats_step(running, block_item):
        row_max, row_total, target_logit = running
        head_block, block_index = block_item
        logits = jnp.dot(head_in, head_block.T, preferred_element_type=jnp.float32)
        vocab_ids = block_index * VOC_DEV + jnp.arange(VOC_DEV, dtype=jnp.int32)
        is_target = vocab_ids[None, :] == targets[:, None]
        new_max = jnp.maximum(row_max, lax.optimization_barrier(jnp.max(logits, axis=1)))
        row_total = row_total * jnp.exp(row_max - new_max) + lax.optimization_barrier(jnp.sum(jnp.exp(logits - new_max[:, None]), axis=1))
        target_logit = target_logit + lax.optimization_barrier(jnp.sum(jnp.where(is_target, logits, 0.0), axis=1))
        return ((new_max, row_total, target_logit), None)
    start_stats = (jnp.full((TOKENS,), -jnp.inf, jnp.float32), jnp.zeros((TOKENS,), jnp.float32), jnp.zeros((TOKENS,), jnp.float32))
    (row_max, row_total, target_logit), _ = lax.scan(stats_step, start_stats, (blocks, indices))
    spread = row_max + jnp.log(row_total)
    loss = spread - target_logit

    def grad_block(block_item):
        head_block, block_index = block_item
        logits = jnp.dot(head_in, head_block.T, preferred_element_type=jnp.float32)
        vocab_ids = block_index * VOC_DEV + jnp.arange(VOC_DEV, dtype=jnp.int32)
        is_target = (vocab_ids[None, :] == targets[:, None]).astype(jnp.float32)
        token_prob = jnp.exp(logits - spread[:, None])
        logit_grad = (loss_weight[:, None] * (token_prob - is_target)).astype(jnp.bfloat16)
        return jnp.dot(logit_grad.T, head_in, preferred_element_type=jnp.float32).astype(jnp.bfloat16)
    head_grad = lax.map(grad_block, (blocks, indices)).reshape(VOCAB, D)
    return (block_out, loss, head_grad)
```

```python
import jax
import jax.numpy as jnp
from jax import lax
from jax.experimental import pallas as pl
from jax.experimental.pallas import tpu as pltpu
from jax.sharding import PartitionSpec as P

BOTH = ("section", "ed")
SIZES = (2, 4, 2, 8, 2)
TOP = 4
CAP = 4
ROWS = 16
N_ED = 32
N_SEC = 8
LANES = 128
F32 = jnp.float32
BF16 = jnp.bfloat16
VMEM_LIMIT = 56 * 1024 * 1024


def pairs_of(move):
    pairs = []
    y_hi_n, x_n, y_lo_n, z_n, core_n = SIZES
    for y_hi in range(y_hi_n):
        for x in range(x_n):
            for y_lo in range(y_lo_n):
                for z in range(z_n):
                    for core in range(core_n):
                        y, x2, z2, core2 = move(y_hi * y_lo_n + y_lo, x, z, core)
                        y, x2, z2 = y % (y_hi_n * y_lo_n), x2 % x_n, z2 % z_n
                        here = (((y_hi * x_n + x) * y_lo_n + y_lo) * z_n + z) * core_n + core
                        there = (
                            ((y // y_lo_n * x_n + x2) * y_lo_n + y % y_lo_n) * z_n + z2
                        ) * core_n + core2
                        pairs.append((here, there))
    return pairs


FROM_Z_UP = pairs_of(lambda y, x, z, c: (y, x, z - 1, c))
FROM_Z_DOWN = pairs_of(lambda y, x, z, c: (y, x, z + 1, c))
FROM_Y_UP = pairs_of(lambda y, x, z, c: (y - 1, x, z, c))
FROM_Y_DOWN = pairs_of(lambda y, x, z, c: (y + 1, x, z, c))
FROM_CORE = pairs_of(lambda y, x, z, c: (y, x, z, 1 - c))


def take(value, pairs):
    return lax.ppermute(value, BOTH, pairs)


OWN_PLACES = [(0, 0), (1, 0), (7, 0), (0, 1), (2, 0), (6, 0), (1, 1), (7, 1)]
OWN_PLACES += [(3, 0), (5, 0), (2, 1), (6, 1), (4, 0), (3, 1), (5, 1), (4, 1)]
PLACES = [(z, y, core) for core in (0, 1) for z, y in OWN_PLACES]


def gather_ed(block):
    up, down = {0: block}, {0: block}
    got = {(0, 0): block}
    for step in (1, 2, 3, 4):
        up[step] = got[step, 0] = take(up[step - 1], FROM_Z_UP)
        if step < 4:
            down[step] = got[8 - step, 0] = take(down[step - 1], FROM_Z_DOWN)
        if step == 1:
            got[0, 1] = take(block, FROM_Y_UP)
        else:
            got[step - 1, 1] = take(up[step - 1], FROM_Y_UP)
            got[9 - step, 1] = take(down[step - 1], FROM_Y_DOWN)
    got[4, 1] = take(up[4], FROM_Y_DOWN)
    pieces = [got[place] for place in OWN_PLACES]
    return pieces + [take(piece, FROM_CORE) for piece in pieces]


def start_rows(pieces, rows_ref, sems):
    ed = lax.axis_index("ed")
    core, z, y_lo = ed % 2, (ed // 2) % 8, ed // 16
    copies = []
    for k, (dz, dy, dc) in enumerate(PLACES):
        from_y = 1 - y_lo if dy else y_lo
        from_c = 1 - core if dc else core
        start = ((from_y * 8 + (z + dz) % 8) * 2 + from_c) * ROWS
        copy = pltpu.make_async_copy(
            pieces[k], rows_ref.at[pl.ds(pl.multiple_of(start, ROWS), ROWS), :], sems.at[k]
        )
        copy.start()
        copies.append(copy)
    return copies


def dot(a, b, dims=((1,), (0,))):
    return lax.dot_general(a, b, (dims, ((), ())), preferred_element_type=F32)


def expert_kernel(*refs):
    pieces, (gate, up, down, out, rows, gate_up, down_v, sems) = refs[:N_ED], refs[N_ED:]
    copies = start_rows(pieces, rows, sems)
    width = gate.shape[0]
    weight_copies = [
        pltpu.make_async_copy(gate, gate_up.at[:, 0:LANES], sems.at[N_ED]),
        pltpu.make_async_copy(up, gate_up.at[:, LANES : 2 * LANES], sems.at[N_ED + 1]),
    ]
    down_copy = pltpu.make_async_copy(down, down_v, sems.at[N_ED + 2])
    for copy in weight_copies + [down_copy]:
        copy.start()
    for copy in copies + weight_copies:
        copy.wait()
    expert = lax.axis_index("ed").astype(F32)
    tokens = rows.shape[0]
    names = rows[:, width : width + LANES].astype(F32)
    hit = jnp.max(jnp.where(names == expert, 1.0, 0.0), axis=1, keepdims=True)
    row_of = lax.broadcasted_iota(jnp.int32, (tokens, tokens), 0)
    col_of = lax.broadcasted_iota(jnp.int32, (tokens, tokens), 1)
    earlier = jnp.where((row_of // ROWS == col_of // ROWS) & (col_of < row_of), 1.0, 0.0)
    hits = jnp.broadcast_to(hit, (tokens, LANES))
    position = dot(earlier.astype(BF16), hits.astype(BF16))
    slot_base = (lax.broadcasted_iota(jnp.int32, (tokens, LANES), 0) // ROWS * CAP).astype(F32)
    slot = lax.broadcasted_iota(jnp.int32, (tokens, LANES), 1).astype(F32)
    chosen = jnp.where((hits > 0.0) & (slot == slot_base + position), 1.0, 0.0).astype(BF16)
    inner = jnp.zeros((LANES, LANES), F32)
    part = 128
    for k in range(tokens // part):
        cut = slice(k * part, (k + 1) * part)
        both = dot(rows[cut, 0:width], gate_up[...])
        gate_proj, up_proj = both[:, :LANES], both[:, LANES:]
        act = (gate_proj / (1.0 + jnp.exp(-gate_proj)) * up_proj).astype(BF16)
        inner = inner + dot(chosen[cut], act, ((0,), (0,)))
    inner = inner.astype(BF16)
    down_copy.wait()
    chunk = width // N_SEC
    for s in range(N_SEC):
        out[s] = dot(inner, down_v[:, s * chunk : (s + 1) * chunk]).astype(BF16)


def run_expert(pieces, gate, up, down):
    width = gate.shape[0]
    tokens = N_ED * ROWS
    return pl.pallas_call(
        expert_kernel,
        out_shape=jax.ShapeDtypeStruct((N_SEC, N_ED * CAP, width // N_SEC), BF16),
        in_specs=[pl.BlockSpec(memory_space=pl.ANY)] * (N_ED + 3),
        out_specs=pl.BlockSpec(memory_space=pltpu.VMEM),
        scratch_shapes=[
            pltpu.VMEM((tokens, width + LANES), BF16),
            pltpu.VMEM((width, 2 * LANES), BF16),
            pltpu.VMEM((LANES, width), BF16),
            pltpu.SemaphoreType.DMA((N_ED + 3,)),
        ],
        compiler_params=pltpu.CompilerParams(vmem_limit_bytes=VMEM_LIMIT),
        name="expert",
    )(*pieces, gate, up, down)


def logits_kernel(*refs):
    pieces, (table, targets, logits, stats, rows, table_v, sems) = refs[:N_ED], refs[N_ED:]
    copies = start_rows(pieces, rows, sems)
    table_copy = pltpu.make_async_copy(table, table_v, sems.at[N_ED])
    table_copy.start()
    for copy in copies + [table_copy]:
        copy.wait()
    vocab, tokens = logits.shape
    first = (lax.axis_index("section") * N_ED + lax.axis_index("ed")) * vocab
    lines = tokens // LANES
    for k in range(lines):
        cut = slice(k * LANES, (k + 1) * LANES)
        part = dot(table_v[...], rows[cut, :], ((1,), (1,)))
        logits[:, cut] = part
        vocab_ids = first + lax.broadcasted_iota(jnp.int32, part.shape, 0)
        row_max = jnp.max(part, axis=0, keepdims=True)
        stats[k : k + 1, :] = row_max
        stats[lines + k : lines + k + 1, :] = jnp.sum(
            jnp.exp(part - row_max), axis=0, keepdims=True
        )
        stats[2 * lines + k : 2 * lines + k + 1, :] = jnp.sum(
            jnp.where(vocab_ids == targets[:, cut], part, 0.0), axis=0, keepdims=True
        )


def run_logits(pieces, table, targets):
    vocab, width = table.shape
    tokens = N_ED * ROWS
    lines = tokens // LANES
    vmem = pl.BlockSpec(memory_space=pltpu.VMEM)
    return pl.pallas_call(
        logits_kernel,
        out_shape=(
            jax.ShapeDtypeStruct((vocab, tokens), F32),
            jax.ShapeDtypeStruct((3 * lines, LANES), F32),
        ),
        in_specs=[pl.BlockSpec(memory_space=pl.ANY)] * (N_ED + 1) + [vmem],
        out_specs=(vmem, vmem),
        scratch_shapes=[
            pltpu.VMEM((tokens, width), BF16),
            pltpu.VMEM((vocab, width), BF16),
            pltpu.SemaphoreType.DMA((N_ED + 1,)),
        ],
        compiler_params=pltpu.CompilerParams(vmem_limit_bytes=VMEM_LIMIT),
        name="logits",
    )(*pieces, table, targets)


def join_stats(parts):
    lines = parts.shape[1] // 3
    maxima = parts[:, 0:lines]
    row_max = jnp.max(maxima, axis=0)
    total = jnp.sum(parts[:, lines : 2 * lines] * jnp.exp(maxima - row_max[None]), axis=0)
    return row_max, total, jnp.sum(parts[:, 2 * lines :], axis=0)


def join_kernel(parts, out):
    lines = parts.shape[1] // 3
    row_max, total, target = join_stats(parts[...])
    for k in range(out.shape[0]):
        out[k, 0:lines] = row_max
        out[k, lines : 2 * lines] = total
        out[k, 2 * lines : 3 * lines] = target


def run_join(parts, copies):
    return pl.pallas_call(
        join_kernel,
        out_shape=jax.ShapeDtypeStruct((copies,) + parts.shape[1:], F32),
        in_specs=[pl.BlockSpec(memory_space=pltpu.VMEM)],
        out_specs=pl.BlockSpec(memory_space=pltpu.VMEM),
        name="join",
    )(parts)


def grad_kernel(*refs):
    pieces = refs[:N_ED]
    parts, logits, targets, weight, loss, grad, rows, sems = refs[N_ED:]
    copies = start_rows(pieces, rows, sems)
    vocab, tokens = logits.shape
    first = (lax.axis_index("section") * N_ED + lax.axis_index("ed")) * vocab
    row_max, total, target = join_stats(parts[...])
    spread = row_max + jnp.log(total)
    loss[...] = spread - target
    for copy in copies:
        copy.wait()
    lines = []
    for k in range(tokens // LANES):
        cut = slice(k * LANES, (k + 1) * LANES)
        part = logits[:, cut]
        vocab_ids = first + lax.broadcasted_iota(jnp.int32, part.shape, 0)
        prob = jnp.exp(part - spread[k : k + 1, :])
        hot = jnp.where(vocab_ids == targets[:, cut], 1.0, 0.0)
        lines.append((weight[:, cut] * (prob - hot)).astype(BF16))
    logit_grad = jnp.concatenate(lines, axis=1)
    width = rows.shape[1]
    step = 1024
    for k in range(width // step):
        cut = slice(k * step, (k + 1) * step)
        grad[:, cut] = dot(logit_grad, rows[:, cut]).astype(BF16)


def run_grad(pieces, parts, logits, targets, weight, width):
    vocab, tokens = logits.shape
    vmem = pl.BlockSpec(memory_space=pltpu.VMEM)
    return pl.pallas_call(
        grad_kernel,
        out_shape=(
            jax.ShapeDtypeStruct((tokens // LANES, LANES), F32),
            jax.ShapeDtypeStruct((vocab, width), BF16),
        ),
        in_specs=[pl.BlockSpec(memory_space=pl.ANY)] * N_ED + [vmem] * 4,
        out_specs=(vmem, vmem),
        scratch_shapes=[
            pltpu.VMEM((tokens, width), BF16),
            pltpu.SemaphoreType.DMA((N_ED,)),
        ],
        compiler_params=pltpu.CompilerParams(vmem_limit_bytes=VMEM_LIMIT),
        name="head_grad",
    )(*pieces, parts, logits, targets, weight)


def rms_scale(values, gain_vec):
    values = values.astype(F32)
    mean_square = jnp.mean(values * values, axis=-1, keepdims=True)
    return values * lax.rsqrt(mean_square + 1e-06) * gain_vec.astype(F32)


def blend_of(expert_ids, gate_weights):
    rows, top = expert_ids.shape
    experts = jnp.arange(N_ED, dtype=jnp.int32)
    named = jnp.any(expert_ids[:, :, None] == experts, axis=1).astype(jnp.int32)
    before = jnp.cumsum(named, axis=0) - named
    slots = jnp.arange(N_ED * CAP, dtype=jnp.int32)
    slot_expert, slot_at = slots // CAP, slots % CAP
    at = jnp.repeat(before, CAP, axis=1) == slot_at[None, :]
    weight = jnp.sum(
        jnp.where(expert_ids[:, :, None] == slot_expert, gate_weights[:, :, None], 0.0), axis=1
    )
    return jnp.where(at, weight, 0.0)


def local(
    hidden,
    moe_gain,
    expert_ids,
    gate_weights,
    gate_matrix,
    up_matrix,
    down_matrix,
    head_gain,
    head_table,
    targets,
    loss_weight,
):
    rows, width = hidden.shape
    chunk = width // N_SEC
    tokens = targets.shape[0]
    normed = rms_scale(hidden, moe_gain).astype(BF16)
    names = jnp.pad(expert_ids.astype(BF16), ((0, 0), (0, LANES - TOP)), constant_values=-1.0)
    pieces = gather_ed(jnp.concatenate([normed, names], axis=1))
    shares = run_expert(pieces, gate_matrix[0], up_matrix[0], down_matrix[0])
    shares = lax.all_to_all(shares, "section", 0, 0, tiled=True)
    summed = jnp.sum(shares.astype(F32), axis=0).astype(BF16).reshape(N_ED, CAP, chunk)
    returned = lax.all_to_all(summed, "ed", 0, 0, tiled=True).reshape(N_ED * CAP, chunk)
    routed = jnp.dot(
        blend_of(expert_ids, gate_weights),
        returned.astype(F32),
        precision=lax.Precision.HIGHEST,
        preferred_element_type=F32,
    )
    section = lax.axis_index("section")
    own = lax.dynamic_slice_in_dim(hidden, section * chunk, chunk, axis=1)
    block_part = (own.astype(F32) + routed).astype(BF16)
    block_all = lax.all_to_all(
        jnp.broadcast_to(block_part[None], (N_SEC, rows, chunk)), "section", 0, 0, tiled=True
    )
    block_out = block_all.transpose(1, 0, 2).reshape(rows, width)
    head_in = rms_scale(block_out, head_gain).astype(BF16)
    pieces = gather_ed(head_in)
    targets_row, weight_row = targets.reshape(1, tokens), loss_weight.reshape(1, tokens)
    logits, stats = run_logits(pieces, head_table, targets_row)
    parts = lax.all_to_all(
        jnp.broadcast_to(stats[None], (N_SEC,) + stats.shape), "section", 0, 0, tiled=True
    )
    parts = lax.all_to_all(run_join(parts, N_ED), "ed", 0, 0, tiled=True)
    loss, head_grad = run_grad(pieces, parts, logits, targets_row, weight_row, width)
    return block_out, loss.reshape(tokens), head_grad


def solution(mesh):
    placed = (
        P("ed", None),
        P(),
        P("ed", None),
        P("ed", None),
        P("ed", None, "section"),
        P("ed", None, "section"),
        P("ed", "section", None),
        P(),
        P(("section", "ed"), None),
        P(),
        P(),
    )
    return jax.shard_map(
        local,
        mesh=mesh,
        in_specs=placed,
        out_specs=(P("ed", None), P(), P(("section", "ed"), None)),
        check_vma=False,
    )
```

```python
import jax
import jax.numpy as jnp
from jax import lax
from jax.experimental import pallas as pl
from jax.experimental.pallas import tpu as pltpu
from jax.sharding import Mesh
from jax.sharding import PartitionSpec as P

AXES = ("y_hi", "x", "y_lo", "z", "core")
SIZES = (2, 4, 2, 8, 2)
SECTION = ("y_hi", "x")
ED = ("y_lo", "z", "core")
CHIP = ("y_lo", "z")
SECTION_CORE = SECTION + ("core",)
TOP = 4
CAP = 4
ROWS = 16
N_ED = 32
N_SEC = 8
N_X = 4
LANES = 128
PARTS = 2
OUT_PARTS = 4
F32 = jnp.float32
BF16 = jnp.bfloat16
VMEM_LIMIT = 58 * 1024 * 1024


def pairs_of(move):
    pairs = []
    y_hi_n, x_n, y_lo_n, z_n, core_n = SIZES
    for y_hi in range(y_hi_n):
        for x in range(x_n):
            for y_lo in range(y_lo_n):
                for z in range(z_n):
                    for core in range(core_n):
                        y, x2, z2, core2 = move(y_hi * y_lo_n + y_lo, x, z, core)
                        y, x2, z2 = y % (y_hi_n * y_lo_n), x2 % x_n, z2 % z_n
                        here = (((y_hi * x_n + x) * y_lo_n + y_lo) * z_n + z) * core_n + core
                        there = (
                            ((y // y_lo_n * x_n + x2) * y_lo_n + y % y_lo_n) * z_n + z2
                        ) * core_n + core2
                        pairs.append((here, there))
    return pairs


FROM_Z = pairs_of(lambda y, x, z, c: (y, x, z - 1 + 2 * c, c))
FROM_Y = pairs_of(lambda y, x, z, c: (y - 1 + 2 * c, x, z, c))
FROM_CORE = pairs_of(lambda y, x, z, c: (y, x, z, 1 - c))
FROM_Y_HI = pairs_of(lambda y, x, z, c: (y + 2, x, z, c))
FROM_X = [pairs_of(lambda y, x, z, c, d=d: (y, x - d, z, c)) for d in range(N_X)]


def take(value, pairs):
    return lax.ppermute(value, AXES, pairs)


RING = [(k, y, 2 * ROWS if 0 < k < 4 else ROWS) for y in (0, 1) for k in (0, 1, 2, 3, 4)]
PLACES = [(0, 0, 0, 2 * ROWS)]
PLACES += [(k, y, swap, n) for swap in (0, 1) for k, y, n in RING if (k, y) != (0, 0)]
N_PIECES = len(PLACES)


def own_rows(block):
    return lax.dynamic_slice_in_dim(block, lax.axis_index("core") * ROWS, ROWS, axis=0)


def gather_ed(block, own):
    z1 = take(block, FROM_Z)
    y0 = take(own, FROM_Y)
    z2 = take(z1, FROM_Z)
    y1 = take(z1, FROM_Y)
    z3 = take(z2, FROM_Z)
    y2 = take(z2, FROM_Y)
    z4 = take(own_rows(z3), FROM_Z)
    y3 = take(z3, FROM_Y)
    y4 = take(z4, FROM_Y)
    ring = [z1, z2, z3, z4, y0, y1, y2, y3, y4]
    return [block] + ring + [take(piece, FROM_CORE) for piece in ring]


CHUNKS = [(0, 0), (0, 1), (1, 0), (3, 0), (2, 0), (1, 1), (3, 1), (2, 1)]


def gather_section(part):
    got = {(0, 0): part, (0, 1): take(part, FROM_Y_HI)}
    for d in (1, 3, 2):
        got[d, 0] = take(part, FROM_X[d])
    got[2, 1] = take(got[2, 0], FROM_Y_HI)
    for d in (1, 3):
        got[d, 1] = take(got[0, 1], FROM_X[d])
    return [got[chunk] for chunk in CHUNKS]


def chunk_start(chunk, steps=0, other=0):
    x, y_hi = lax.axis_index("x"), lax.axis_index("y_hi")
    from_y = 1 - y_hi if other else y_hi
    return ((x + steps) % N_X * 2 + from_y) * chunk


def column_cuts(width):
    part = width // (PARTS * LANES) * LANES
    first = width - part * (PARTS - 1)
    return [(0, first)] + [(first + p * part, part) for p in range(PARTS - 1)]


def start_rows(pieces, rows_ref, sems):
    core, z, y_lo = lax.axis_index("core"), lax.axis_index("z"), lax.axis_index("y_lo")
    all_copies = []
    for p, (at, size) in enumerate(column_cuts(rows_ref.shape[1])):
        copies = []
        for k, (step, other_y, swap, n) in enumerate(PLACES):
            ring = 1 - core if swap else core
            from_z = (z + step + 8 * ring - 2 * step * ring) % 8
            from_y = 1 - y_lo if other_y else y_lo
            start = (from_y * 8 + from_z) * 2 * ROWS
            if n == ROWS:
                start = start + ring * ROWS
            copy = pltpu.make_async_copy(
                pieces[k].at[:, pl.ds(at, size)],
                rows_ref.at[pl.ds(pl.multiple_of(start, ROWS), n), pl.ds(at, size)],
                sems.at[p, k],
            )
            copy.start()
            copies.append(copy)
        all_copies.append(copies)
    return all_copies


def dot(a, b, dims=((1,), (0,))):
    return lax.dot_general(a, b, (dims, ((), ())), preferred_element_type=F32)


def expert_index():
    return (lax.axis_index("y_lo") * 8 + lax.axis_index("z")) * 2 + lax.axis_index("core")


def dispatch_kernel(hidden, ids, weights, gain, down, slots, blend, *refs):
    quarters, (normed, sems) = refs[:N_X], refs[N_X:]
    width = hidden.shape[1]
    quarter, chunk = width // N_X, width // N_SEC
    x = lax.axis_index("x")
    copies = []
    for d in range(N_X):
        start = pl.multiple_of((x + N_X - d) % N_X * quarter, LANES)
        copy = pltpu.make_async_copy(
            down.at[:, pl.ds(start, quarter)], quarters[d], sems.at[d]
        )
        copy.start()
        copies.append(copy)
    value = hidden[...].astype(F32)
    scale = lax.rsqrt(jnp.mean(value * value, axis=-1, keepdims=True) + 1e-06)
    normed[...] = (value * scale * gain[...].astype(F32).reshape(1, width)).astype(BF16)
    slot = lax.broadcasted_iota(jnp.int32, (N_ED * CAP, ROWS), 0)
    hit = jnp.zeros((N_ED * CAP, ROWS), F32)
    weight = jnp.zeros((N_ED * CAP, ROWS), F32)
    for k in range(TOP):
        named = ids[k : k + 1, :] == slot // CAP
        hit = jnp.where(named, 1.0, hit)
        weight = jnp.where(named, weights[k : k + 1, :], weight)
    row_of = lax.broadcasted_iota(jnp.int32, (ROWS, ROWS), 0)
    col_of = lax.broadcasted_iota(jnp.int32, (ROWS, ROWS), 1)
    before = dot(hit.astype(BF16), jnp.where(row_of < col_of, 1.0, 0.0).astype(BF16))
    placed = (hit > 0.0) & (before == (slot % CAP).astype(F32))
    blend[...] = jnp.where(placed, weight, 0.0)
    own = normed[:, pl.ds(pl.multiple_of(chunk_start(chunk), LANES), chunk)]
    slots[...] = dot(jnp.where(placed, 1.0, 0.0).astype(BF16), own).astype(BF16)
    for copy in copies:
        copy.wait()


def run_dispatch(hidden, ids, weights, gain, down):
    rows, width = hidden.shape
    quarter = jax.ShapeDtypeStruct((down.shape[0], width // N_X), BF16)
    vmem = pl.BlockSpec(memory_space=pltpu.VMEM)
    hbm = pl.BlockSpec(memory_space=pltpu.HBM)
    outs = pl.pallas_call(
        dispatch_kernel,
        out_shape=[
            jax.ShapeDtypeStruct((N_ED * CAP, width // N_SEC), BF16),
            jax.ShapeDtypeStruct((N_ED * CAP, rows), F32),
        ]
        + [quarter] * N_X,
        in_specs=[vmem] * 4 + [hbm],
        out_specs=[vmem] * (2 + N_X),
        scratch_shapes=[pltpu.VMEM((rows, width), BF16), pltpu.SemaphoreType.DMA((N_X,))],
        compiler_params=pltpu.CompilerParams(vmem_limit_bytes=16 * 1024 * 1024),
        name="dispatch",
    )(hidden, ids, weights, gain, down)
    return outs[0], outs[1], outs[2:]


def row_shapes(width):
    return [jax.ShapeDtypeStruct((n * ROWS, width), BF16) for n in (2, 1)]


def run_pack(own, other, own_names, other_names, gain):
    vmem = pl.BlockSpec(memory_space=pltpu.VMEM)
    return pl.pallas_call(
        pack_kernel,
        out_shape=row_shapes(own.shape[1] + LANES),
        in_specs=[vmem] * 5,
        out_specs=[vmem] * 2,
        name="pack",
    )(own, other, own_names, other_names, gain)


def head_kernel(chunks, gain, block_out, block, alone):
    core = lax.axis_index("core")
    chunk = chunks.shape[2]
    width = N_SEC * chunk
    gains = gain[...].astype(F32).reshape(1, width)
    for k in range(2):
        of_core = core if k == 0 else 1 - core
        rows = pl.ds(pl.multiple_of(of_core * ROWS, ROWS), ROWS)
        square = jnp.zeros((ROWS, 1), F32)
        for s in range(N_SEC):
            value = chunks[2 * s + of_core].astype(F32)
            square = square + jnp.sum(value * value, axis=-1, keepdims=True)
        scale = lax.rsqrt(square / width + 1e-06)
        for s in range(N_SEC):
            at = (s % N_X * 2 + s // N_X) * chunk
            cut = slice(at, at + chunk)
            own = chunks[2 * s + of_core]
            normed = (own.astype(F32) * scale * gains[:, cut]).astype(BF16)
            block[rows, cut] = normed
            if k == 0:
                alone[:, cut] = normed
                block_out[:, cut] = own


def run_head(chunks, gain):
    width = N_SEC * chunks.shape[2]
    vmem = pl.BlockSpec(memory_space=pltpu.VMEM)
    return pl.pallas_call(
        head_kernel,
        out_shape=[jax.ShapeDtypeStruct((ROWS, width), BF16)] + row_shapes(width),
        in_specs=[vmem] * 2,
        out_specs=[vmem] * 3,
        name="head_norm",
    )(chunks, gain)


def inner_kernel(*refs):
    pieces, (gate, up, out, gate_up, sems) = refs[:N_SEC], refs[N_SEC:]
    chunk = pieces[0].shape[1]
    copies = []
    for k, (steps, other) in enumerate(CHUNKS):
        rows = pl.ds(pl.multiple_of(chunk_start(chunk, steps, other), LANES), chunk)
        for j, weight in enumerate((gate, up)):
            copy = pltpu.make_async_copy(
                weight.at[rows, :], gate_up.at[k, :, pl.ds(j * LANES, LANES)], sems.at[2 * k + j]
            )
            copy.start()
            copies.append(copy)
    total = None
    for k in range(N_SEC):
        copies[2 * k].wait()
        copies[2 * k + 1].wait()
        product = dot(pieces[k][...], gate_up[k])
        total = product if total is None else total + product
    gate_proj, up_proj = total[:, :LANES], total[:, LANES:]
    out[...] = (gate_proj / (1.0 + jnp.exp(-gate_proj)) * up_proj).astype(BF16)


def run_inner(pieces, gate, up):
    vmem = pl.BlockSpec(memory_space=pltpu.VMEM)
    hbm = pl.BlockSpec(memory_space=pltpu.HBM)
    slots, chunk = pieces[0].shape
    return pl.pallas_call(
        inner_kernel,
        out_shape=jax.ShapeDtypeStruct((slots, LANES), BF16),
        in_specs=[vmem] * N_SEC + [hbm] * 2,
        out_specs=vmem,
        scratch_shapes=[
            pltpu.VMEM((N_SEC, chunk, 2 * LANES), BF16),
            pltpu.SemaphoreType.DMA((2 * N_SEC,)),
        ],
        compiler_params=pltpu.CompilerParams(vmem_limit_bytes=VMEM_LIMIT),
        name="inner",
    )(*pieces, gate, up)


def down_kernel(*refs):
    inner, down, (keep, send, total) = refs[:N_X], refs[N_X : 2 * N_X], refs[2 * N_X :]
    acc = dot(inner[0][...], down[0][...])
    for d in range(1, N_X):
        acc = acc + dot(inner[d][...], down[d][...])
    total[...] = acc
    chunk = keep.shape[1]
    y_hi = lax.axis_index("y_hi")
    keep[...] = total[:, pl.ds(pl.multiple_of(y_hi * chunk, LANES), chunk)]
    send[...] = total[:, pl.ds(pl.multiple_of((1 - y_hi) * chunk, LANES), chunk)].astype(BF16)


def run_down(inner, down):
    slots, quarter = inner[0].shape[0], down[0].shape[1]
    vmem = pl.BlockSpec(memory_space=pltpu.VMEM)
    return pl.pallas_call(
        down_kernel,
        out_shape=(
            jax.ShapeDtypeStruct((slots, quarter // 2), F32),
            jax.ShapeDtypeStruct((slots, quarter // 2), BF16),
        ),
        in_specs=[vmem] * (2 * N_X),
        out_specs=(vmem, vmem),
        scratch_shapes=[pltpu.VMEM((slots, quarter), F32)],
        compiler_params=pltpu.CompilerParams(vmem_limit_bytes=VMEM_LIMIT),
        name="down",
    )(*inner, *down)


def vocab_start(vocab):
    section = lax.axis_index("y_hi") * N_X + lax.axis_index("x")
    return (section * N_ED + expert_index()) * vocab


def logits_kernel(*refs):
    pieces, (table, targets, logits, stats, gathered, rows, table_v, sems, table_sems) = (
        refs[:N_PIECES],
        refs[N_PIECES:],
    )
    vocab, tokens = logits.shape
    part = table.shape[1] // PARTS
    table_copies = []
    for p in range(PARTS):
        cut = pl.ds(p * part, part)
        copy = pltpu.make_async_copy(table.at[:, cut], table_v.at[:, cut], table_sems.at[p])
        copy.start()
        table_copies.append(copy)
    copies = start_rows(pieces, rows, sems)
    out_copies = []
    for p in range(PARTS):
        for copy in [table_copies[p]] + copies[p]:
            copy.wait()
        out_cut = pl.ds(p * part, part)
        out_copies.append(
            pltpu.make_async_copy(
                rows.at[:, out_cut], gathered.at[:, out_cut], table_sems.at[PARTS + p]
            )
        )
        out_copies[p].start()
        cut = slice(p * part, (p + 1) * part)
        product = dot(table_v[:, cut], rows[:, cut], ((1,), (1,)))
        if p == 0:
            logits[...] = product
        else:
            logits[...] += product
    first = vocab_start(vocab)
    lines = tokens // LANES
    found = [[], [], []]
    for k in range(lines):
        cut = slice(k * LANES, (k + 1) * LANES)
        value = logits[:, cut]
        vocab_ids = first + lax.broadcasted_iota(jnp.int32, value.shape, 0)
        row_max = jnp.max(value, axis=0, keepdims=True)
        hot = vocab_ids == targets[:, cut]
        found[0].append(row_max)
        found[1].append(jnp.sum(jnp.exp(value - row_max), axis=0, keepdims=True))
        found[2].append(jnp.sum(jnp.where(hot, value, 0.0), axis=0, keepdims=True))
    spread_out([jnp.concatenate(values, axis=0) for values in found], stats)
    for copy in out_copies:
        copy.wait()


def run_logits(pieces, table, targets):
    vocab, width = table.shape
    tokens = N_ED * ROWS
    lines = tokens // LANES
    vmem = pl.BlockSpec(memory_space=pltpu.VMEM)
    hbm = pl.BlockSpec(memory_space=pltpu.HBM)
    return pl.pallas_call(
        logits_kernel,
        out_shape=(
            jax.ShapeDtypeStruct((vocab, tokens), F32),
            jax.ShapeDtypeStruct((2 * N_SEC, 3 * lines, LANES), F32),
            jax.ShapeDtypeStruct((tokens, width), BF16),
        ),
        in_specs=[pl.BlockSpec(memory_space=pl.ANY)] * N_PIECES + [hbm, vmem],
        out_specs=(vmem, vmem, hbm),
        scratch_shapes=[
            pltpu.VMEM((tokens, width), BF16),
            pltpu.VMEM((vocab, width), BF16),
            pltpu.SemaphoreType.DMA((PARTS, N_PIECES)),
            pltpu.SemaphoreType.DMA((2 * PARTS,)),
        ],
        compiler_params=pltpu.CompilerParams(vmem_limit_bytes=VMEM_LIMIT),
        name="logits",
    )(*pieces, table, targets)


def join_stats(parts):
    lines = parts.shape[1] // 3
    maxima = parts[:, 0:lines]
    row_max = jnp.max(maxima, axis=0)
    total = jnp.sum(parts[:, lines : 2 * lines] * jnp.exp(maxima - row_max[None]), axis=0)
    return row_max, total, jnp.sum(parts[:, 2 * lines :], axis=0)


def spread_out(stats, out):
    row_max, total, target = stats
    lines = row_max.shape[0]
    for k in range(out.shape[0]):
        out[k, 0:lines] = row_max
        out[k, lines : 2 * lines] = total
        out[k, 2 * lines : 3 * lines] = target


def join_kernel(parts, out):
    spread_out(join_stats(parts[...]), out)


def run_join(kernel, operands, shape):
    vmem = pl.BlockSpec(memory_space=pltpu.VMEM)
    return pl.pallas_call(
        kernel,
        out_shape=jax.ShapeDtypeStruct(shape, F32),
        in_specs=[vmem] * len(operands),
        out_specs=vmem,
        name="join",
    )(*operands)


def grad_kernel(gathered, parts, logits, targets, weight, loss, grad, rows, grad_v, sems):
    vocab, tokens = logits.shape
    part = rows.shape[1] // OUT_PARTS
    in_copies = []
    for p in range(OUT_PARTS):
        cut = pl.ds(p * part, part)
        copy = pltpu.make_async_copy(gathered.at[:, cut], rows.at[:, cut], sems.at[p])
        copy.start()
        in_copies.append(copy)
    first = vocab_start(vocab)
    row_max, total, target = join_stats(parts[...])
    spread = row_max + jnp.log(total)
    loss[...] = spread - target
    lines = []
    for k in range(tokens // LANES):
        cut = slice(k * LANES, (k + 1) * LANES)
        vocab_ids = first + lax.broadcasted_iota(jnp.int32, (vocab, LANES), 0)
        prob = jnp.exp(logits[:, cut] - spread[k : k + 1, :])
        hot = jnp.where(vocab_ids == targets[:, cut], 1.0, 0.0)
        lines.append((weight[:, cut] * (prob - hot)).astype(BF16))
    logit_grad = jnp.concatenate(lines, axis=1)
    out_copies = []
    for p in range(OUT_PARTS):
        in_copies[p].wait()
        cut = slice(p * part, (p + 1) * part)
        grad_v[p] = dot(logit_grad, rows[:, cut]).astype(BF16)
        copy = pltpu.make_async_copy(
            grad_v.at[p], grad.at[:, pl.ds(p * part, part)], sems.at[OUT_PARTS + p]
        )
        copy.start()
        out_copies.append(copy)
    for copy in out_copies:
        copy.wait()


def run_grad(gathered, parts, logits, targets, weight):
    (vocab, tokens), width = logits.shape, gathered.shape[1]
    vmem = pl.BlockSpec(memory_space=pltpu.VMEM)
    hbm = pl.BlockSpec(memory_space=pltpu.HBM)
    return pl.pallas_call(
        grad_kernel,
        out_shape=(
            jax.ShapeDtypeStruct((tokens // LANES, LANES), F32),
            jax.ShapeDtypeStruct((vocab, width), BF16),
        ),
        in_specs=[hbm] + [vmem] * 4,
        out_specs=(vmem, hbm),
        scratch_shapes=[
            pltpu.VMEM((tokens, width), BF16),
            pltpu.VMEM((OUT_PARTS, vocab, width // OUT_PARTS), BF16),
            pltpu.SemaphoreType.DMA((2 * OUT_PARTS,)),
        ],
        compiler_params=pltpu.CompilerParams(vmem_limit_bytes=VMEM_LIMIT),
        name="head_grad",
    )(gathered, parts, logits, targets, weight)


def local(
    hidden,
    moe_gain,
    expert_ids,
    gate_weights,
    gate_matrix,
    up_matrix,
    down_matrix,
    head_gain,
    head_table,
    targets,
    loss_weight,
):
    rows, width = hidden.shape
    chunk = width // N_SEC
    tokens = targets.shape[0]
    slots, blend, down = run_dispatch(
        hidden, expert_ids.T, gate_weights.T, moe_gain, down_matrix[0]
    )
    down = [take(part, FROM_X[d]) if d else part for d, part in enumerate(down)]
    arrived = lax.all_to_all(slots.reshape(N_ED, CAP, chunk), ED, 0, 0, tiled=True)
    arrived, down = lax.optimization_barrier((arrived, down))
    pieces = gather_section(arrived.reshape(N_ED * CAP, chunk))
    inner = run_inner(pieces, gate_matrix[0], up_matrix[0])
    inner = [take(inner, FROM_X[d]) if d else inner for d in range(N_X)]
    keep, send = run_down(inner, down)
    summed = (keep + take(send, FROM_Y_HI).astype(F32)).astype(BF16)
    returned = lax.all_to_all(summed.reshape(N_ED, CAP, chunk), ED, 0, 0, tiled=True)
    routed = lax.dot_general(
        blend,
        returned.reshape(N_ED * CAP, chunk).astype(F32),
        (((0,), (0,)), ((), ())),
        precision=lax.Precision.HIGHEST,
        preferred_element_type=F32,
    )
    own = lax.dynamic_slice_in_dim(hidden, chunk_start(chunk), chunk, axis=1)
    block_part = (own.astype(F32) + routed).astype(BF16)
    chunks = lax.all_to_all(
        jnp.broadcast_to(block_part[None], (2 * N_SEC, rows, chunk)),
        SECTION_CORE,
        0,
        0,
        tiled=True,
    )
    block_out, block, own = run_head(chunks, head_gain)
    pieces = gather_ed(block, own)
    targets_row, weight_row = targets.reshape(1, tokens), loss_weight.reshape(1, tokens)
    logits, stats, gathered = run_logits(pieces, head_table, targets_row)
    parts = lax.all_to_all(stats, SECTION_CORE, 0, 0, tiled=True)
    parts = run_join(join_kernel, (parts,), (N_ED // 2,) + stats.shape[1:])
    parts = lax.all_to_all(parts, CHIP, 0, 0, tiled=True)
    loss, head_grad = run_grad(gathered, parts, logits, targets_row, weight_row)
    return block_out, loss.reshape(tokens), head_grad


def solution(mesh):
    fine = Mesh(mesh.devices.reshape(SIZES), AXES)
    placed = (
        P(ED, None),
        P(),
        P(ED, None),
        P(ED, None),
        P(ED, None, SECTION),
        P(ED, None, SECTION),
        P(ED, SECTION, None),
        P(),
        P(SECTION + ED, None),
        P(),
        P(),
    )
    return jax.shard_map(
        local,
        mesh=fine,
        in_specs=placed,
        out_specs=(P(ED, None), P(), P(SECTION + ED, None)),
        check_vma=False,
    )
```
